256 devices in a mesh: req: 2 (over y_lo), ctx: 16 (over z, core), tp: 8 (over x, y_hi).
Axes of the slice: x: 4, y: 4 (y_hi: 2, y_lo: 2; y = y_hi * 2 + y_lo), z: 8, core: 2. Of those that a mesh axis runs over, the one named last changes fastest.
Arguments:
- queries: bfloat16 [1024, 16384], P(('req', 'ctx'), 'tp'), parts along dimension 0, may hold values from -200 to 200, as said below
- new_keys: bfloat16 [1024, 1024], P(('req', 'ctx'), 'tp'), parts along dimension 0, may hold values from -8 to 8, as said below
- fresh_values: bfloat16 [1024, 1024], P(('req', 'ctx'), 'tp'), parts along dimension 0, may hold values from -6 to 6
- history_keys: bfloat16 [65536, 1024], P(('req', 'ctx'), 'tp'), parts along dimension 0, may hold values from -6 to 6
- history_values: bfloat16 [65536, 1024], P(('req', 'ctx'), 'tp'), parts along dimension 0, may hold values from -6 to 6
- hist_lens: int32 [8], P('req'), parts along dimension 0, may hold values from 1 to 16384, 32768 in all
- new_lens: int32 [8], P('req'), parts along dimension 0, may hold values from 1 to 256, 512 in all
Outputs:
- attended: bfloat16 [1024, 16384], P(('req', 'ctx'), 'tp'), parts along dimension 0
The draws below stay inside these ranges and needn't reach their ends.
There are 2 independent parts, one for each index of `req`. The reference program is written for one: setup_inputs(seed, part) draws one part's arguments, and reference() takes and returns one part's arrays. A program takes and returns all parts, laid end to end along the dimension named above; each array names one. Nothing has to cross between parts.
Inputs may be any that keep to these rules, and one draw needn't show every extreme that they name: Custom queries. `new_keys`: any values in the stated range. `hist_lens`: every request holds at least one history position; the largest holds exactly 16384. `new_lens`: every request holds at least one new token; the largest holds exactly 256.
All inputs are finite; a program needn't handle non-finite values.
Results may differ from the reference program's by a relative error of at most 0.018.
Values may be sent and summed in bfloat16 or wider, within the bound.
No kernel may reach another device: no remote copies, remote signals or barrier semaphores. Data moves between devices by JAX's collectives and lax.ppermute only.
A program may use at most 64 MiB of HBM per device.

```python
import math
import jax
import jax.numpy as jnp
import numpy as np
from jax import lax

QUERY_HEADS = 128
KEY_VALUE_HEADS = 8
HEAD_SIZE = 128
REQS = 4
HISTORY_SLOTS = 32768
FRESH_TOKENS = 512


def shared_keys(key):
    first_entry = jax.random.fold_in(key, 0)
    base_offset = jax.random.normal(first_entry, (FRESH_TOKENS, KEY_VALUE_HEADS * HEAD_SIZE), jnp.float32)
    return base_offset


def merged_keys(base_offset):
    return base_offset


def draw_new_keys(key, part):
    base_offset = shared_keys(key)
    return merged_keys(base_offset).astype(jnp.bfloat16)


def draw_queries(key, part):
    key = jax.random.fold_in(key, 2)
    values = jax.random.normal(key, (FRESH_TOKENS, QUERY_HEADS * HEAD_SIZE), jnp.float32)
    return values.astype(jnp.bfloat16)


def levels(key, dims, cuts, smallest, high):
    def one(axis_at, parts):
        heights = jax.random.uniform(jax.random.fold_in(jax.random.fold_in(key, 6), axis_at), (parts,), jnp.float32, smallest / len(cuts), high / len(cuts))
        return jnp.repeat(jnp.exp(heights), dims[axis_at] // parts).reshape((-1,) + (1,) * (len(dims) - axis_at - 1))

    gain = one(*cuts[0])
    for cut in cuts[1:]:
        gain = gain * one(*cut)
    return gain


def length_profile(number_of, total, limit, slope):
    weights = [(1 << 20) // math.isqrt(rank ** slope) + 1 for rank in range(2, number_of + 1)]
    rest, holding = total - limit - (number_of - 1), [1] * (number_of - 1)
    while rest > 0:
        movable = [i for i in range(number_of - 1) if holding[i] < limit]
        mass, remaining = sum([weights[i] for i in movable]), rest
        for i in movable:
            extra = min(limit - holding[i], max(1, remaining * weights[i] // mass), rest)
            holding[i] = holding[i] + extra
            rest = rest - extra
    return np.array([limit] + holding)


def uneven(rng, number_of, total, limit, skew):
    if number_of == 2:
        one = jax.random.randint(rng, (), max(1, total - limit), min(limit, total - 1) + 1)
        return jnp.stack([one, total - one])
    sizes = jnp.asarray(length_profile(number_of, total, limit, skew), jnp.int32)
    pairs = (number_of - 1) // 2
    giver, sink = sizes[1:1 + 2 * pairs:2], sizes[2:2 + 2 * pairs:2]
    room = jnp.minimum(giver - 1, limit - sink)
    passed = jax.random.randint(jax.random.fold_in(rng, 1), (pairs,), 0, 1 << 20) % (room + 1)
    sizes = sizes.at[1:1 + 2 * pairs:2].set(giver - passed).at[2:2 + 2 * pairs:2].set(sink + passed)
    return sizes[jax.random.permutation(jax.random.fold_in(rng, 2), number_of)]


def gaussian(rng, dims, width, limit, pieces=(), kind=jnp.bfloat16):
    values = width * jax.random.normal(rng, dims, jnp.float32)
    if pieces:
        values = values * levels(rng, dims, pieces, -0.22, 0.18)
    return jnp.clip(values, -limit, limit).astype(kind)


def setup_inputs(seed: int = 0, part: int = 0) -> dict:
    arg_keys = jax.random.split(jax.random.key(seed), 8)
    part_splits = jax.random.split(jax.random.fold_in(arg_keys[7], part), 8)
    queries = draw_queries(jax.random.fold_in(jax.random.fold_in(arg_keys[7], part), 71), part)
    new_keys = draw_new_keys(jax.random.fold_in(jax.random.fold_in(arg_keys[7], part), 71), part)
    fresh_values = gaussian(part_splits[2], (FRESH_TOKENS, KEY_VALUE_HEADS * HEAD_SIZE), 1.0, 6.0, ((0, 16), (1, 8)))
    history_keys = gaussian(part_splits[3], (HISTORY_SLOTS, KEY_VALUE_HEADS * HEAD_SIZE), 1.0, 6.0, ((0, 16), (1, 8)))
    history_values = gaussian(part_splits[4], (HISTORY_SLOTS, KEY_VALUE_HEADS * HEAD_SIZE), 1.0, 6.0, ((0, 16), (1, 8)))
    hist_lens = uneven(part_splits[5], REQS, HISTORY_SLOTS, HISTORY_SLOTS // 2, 2).astype(jnp.int32)
    new_lens = uneven(part_splits[6], REQS, FRESH_TOKENS, FRESH_TOKENS // 2, 2).astype(jnp.int32)
    return dict(queries=queries, new_keys=new_keys, fresh_values=fresh_values, history_keys=history_keys, history_values=history_values, hist_lens=hist_lens, new_lens=new_lens)


NEG = -1.0e30


def segment_of(index, lens):
    ends = jnp.cumsum(lens)
    return jnp.sum((index[:, None] >= ends[None, :]).astype(jnp.int32), axis=1)


def reference(queries, new_keys, fresh_values, history_keys, history_values, hist_lens, new_lens):
    new_count = queries.shape[0]
    hist_count = history_keys.shape[0]
    keys_all = jnp.concatenate([history_keys, new_keys], axis=0)
    values_all = jnp.concatenate([history_values, fresh_values], axis=0)
    qpos = jnp.arange(new_count, dtype=jnp.int32)
    qseg = segment_of(qpos, new_lens)
    hseg = segment_of(jnp.arange(hist_count, dtype=jnp.int32), hist_lens)
    hist_mask = qseg[:, None] == hseg[None, :]
    new_mask = (qseg[:, None] == qseg[None, :]) & (qpos[None, :] <= qpos[:, None])
    mask = jnp.concatenate([hist_mask, new_mask], axis=1)
    scale = HEAD_SIZE ** -0.5

    def one_head(head_index):
        request_group = head_index // (QUERY_HEADS // KEY_VALUE_HEADS)
        query = lax.dynamic_slice_in_dim(queries, (head_index * HEAD_SIZE).astype(jnp.int32), HEAD_SIZE, 1)
        key_rows = lax.dynamic_slice_in_dim(keys_all, (request_group * HEAD_SIZE).astype(jnp.int32), HEAD_SIZE, 1)
        values = lax.dynamic_slice_in_dim(values_all, (request_group * HEAD_SIZE).astype(jnp.int32), HEAD_SIZE, 1)
        scores = jnp.dot(query, key_rows.T, preferred_element_type=jnp.float32) * scale
        scores = jnp.where(mask, scores, NEG)
        top = jnp.max(scores, axis=1)
        weights = jnp.where(mask, jnp.exp(scores - top[:, None]), 0.0)
        total = jnp.sum(weights, axis=1)
        numer = jnp.dot(weights.astype(jnp.bfloat16), values, preferred_element_type=jnp.float32)
        return (numer / total[:, None]).astype(jnp.bfloat16)

    heads = lax.map(one_head, jnp.arange(QUERY_HEADS, dtype=jnp.int32))
    return jnp.transpose(heads, (1, 0, 2)).reshape(new_count, QUERY_HEADS * HEAD_SIZE)
```

```python
import functools
import math

import jax
import jax.numpy as jnp
from jax import lax
from jax.experimental import pallas as pl
from jax.experimental.pallas import tpu as pltpu
from jax.sharding import PartitionSpec as P

HEAD_SIZE = 128
REQS = 4
TILE = 512
STAT_ROWS = 16
LOG2_SCALE = math.log2(math.e) * HEAD_SIZE**-0.5
NEG = -3.0e38
FLOOR = -(2.0**100)


def ends_of(info, first):
    total = info[first]
    ends = [total]
    for r in range(1, REQS):
        total = total + info[first + r]
        ends.append(total)
    return ends


def request_of(position, ends):
    found = jnp.zeros_like(position)
    for end in ends[:-1]:
        found = found + (position >= end).astype(jnp.int32)
    return found


def pick(request, values):
    result = values[0]
    for r in range(1, REQS):
        result = jnp.where(request == r, values[r], result)
    return result


def wide(column_block, width):
    if width <= 128:
        return column_block[:, :width]
    return jnp.concatenate([column_block] * (width // 128), axis=1)


def eye():
    rows = lax.broadcasted_iota(jnp.int32, (128, 128), 0)
    return rows == lax.broadcasted_iota(jnp.int32, (128, 128), 1)


def pack(top, total):
    high = total.astype(jnp.bfloat16).astype(jnp.float32)
    low = (total - high).astype(jnp.bfloat16).astype(jnp.float32)
    groups = top.shape[0] // 128
    diagonal = eye()
    at = lax.broadcasted_iota(jnp.int32, (STAT_ROWS, 128), 0)
    stats = jnp.zeros((STAT_ROWS, 128), jnp.float32)
    for kind, source in enumerate((top, high, low)):
        for g in range(groups):
            piece = source[g * 128 : (g + 1) * 128]
            row = jnp.sum(jnp.where(diagonal, piece, 0.0), axis=0, keepdims=True)
            stats = jnp.where(at == kind * groups + g, row, stats)
    return stats


def unpack(stats, rows):
    groups = rows // 128
    diagonal = eye()
    ones = jnp.ones((128, 128), jnp.bfloat16)

    def spread(i):
        row = jnp.broadcast_to(stats[i : i + 1].astype(jnp.float32), (128, 128))
        masked = jnp.where(diagonal, row, 0.0).astype(jnp.bfloat16)
        return jnp.dot(masked, ones, preferred_element_type=jnp.float32)

    top = jnp.concatenate([spread(g) for g in range(groups)], axis=0)
    total = jnp.concatenate([spread(groups + g) + spread(2 * groups + g) for g in range(groups)], axis=0)
    return top, total


def attend_kernel(shifts, tokens, heads, chips, info_ref, *refs):
    blocks = len(shifts)
    q_refs, refs = refs[:blocks], refs[blocks:]
    keys_refs, values_refs, refs = refs[0:2], refs[2:4], refs[4:]
    new_refs, refs = refs[0:2], refs[2:]
    out_refs, (top_ref, acc_ref) = refs[:blocks], refs[blocks:]
    rows = tokens * heads
    chip, core = info_ref[2 * REQS], info_ref[2 * REQS + 1]
    hist_ends, new_ends = ends_of(info_ref, 0), ends_of(info_ref, REQS)
    hist_starts = [jnp.int32(0)] + hist_ends[:-1]
    span = keys_refs[0].shape[0]

    for shift, q_ref, out_ref in zip(shifts, q_refs, out_refs, strict=True):
        owner = lax.rem(chip + (shift + chips), chips)
        first_token = (owner * 2 + core) * tokens
        low_request = request_of(first_token, new_ends)
        high_request = request_of(first_token + (tokens - 1), new_ends)
        low, high = pick(low_request, hist_starts), pick(high_request, hist_ends)
        token = first_token + lax.broadcasted_iota(jnp.int32, (tokens, 1), 0)
        request = request_of(token, new_ends)
        row_low, row_high = pick(request, hist_starts), pick(request, hist_ends)
        query = jnp.concatenate(
            [q_ref[:, h * HEAD_SIZE : (h + 1) * HEAD_SIZE] for h in range(heads)], axis=0
        )
        top_ref[...] = jnp.full((rows, 128), FLOOR, jnp.float32)
        acc_ref[...] = jnp.zeros((rows, 256), jnp.float32)

        def absorb(keys, values, mask, query=query):
            count = keys.shape[0]
            scores = lax.dot_general(query, keys, (((1,), (1,)), ((), ())), preferred_element_type=jnp.float32)
            scores = scores * LOG2_SCALE
            if mask is not None:
                scores = jnp.where(mask[None], scores.reshape(heads, tokens, count), NEG).reshape(rows, count)
            most = jnp.max(scores, axis=1, keepdims=True)
            old = top_ref[...]
            new = jnp.maximum(old, most.astype(jnp.bfloat16).astype(jnp.float32))
            weights = jnp.exp2(scores - wide(new, count)).astype(jnp.bfloat16)
            shrink = jnp.exp2(old - new)
            both = jnp.concatenate([values, jnp.ones((count, 128), jnp.bfloat16)], axis=1)
            acc_ref[...] = acc_ref[...] * wide(shrink, 256) + jnp.dot(
                weights, both, preferred_element_type=jnp.float32
            )
            top_ref[...] = new

        for half in range(2):
            base = (chip * 2 + (core if half == 0 else 1 - core)) * span
            begin = jnp.clip(lax.div(jnp.maximum(low - base, 0), TILE), 0, span // TILE)
            end = jnp.clip(lax.div(jnp.maximum(high - base, 0) + (TILE - 1), TILE), 0, span // TILE)

            def tile(i, unused, half=half, base=base):
                at = pl.multiple_of(i * TILE, TILE)
                first = base + i * TILE
                whole = (low_request == high_request) & (first >= low) & (first + TILE <= high)

                @pl.when(whole)
                def _():
                    absorb(keys_refs[half][pl.ds(at, TILE)], values_refs[half][pl.ds(at, TILE)], None)

                @pl.when(jnp.logical_not(whole))
                def _():
                    position = first + lax.broadcasted_iota(jnp.int32, (tokens, TILE), 1)
                    mask = (position >= row_low) & (position < row_high)
                    absorb(keys_refs[half][pl.ds(at, TILE)], values_refs[half][pl.ds(at, TILE)], mask)

                return unused

            lax.fori_loop(begin, end, tile, 0)

        chip_first = chip * (2 * tokens)
        chip_low = request_of(chip_first, new_ends)
        chip_high = request_of(chip_first + (2 * tokens - 1), new_ends)

        @pl.when((owner >= chip) & (chip_low <= high_request) & (chip_high >= low_request))
        def _():
            for half in range(2):
                first = (chip * 2 + (core if half == 0 else 1 - core)) * tokens
                position = first + lax.broadcasted_iota(jnp.int32, (tokens, tokens), 1)
                mask = (position <= token) & (request_of(position, new_ends) == request)
                absorb(new_refs[half][:tokens], new_refs[half][tokens:], mask)

        acc = acc_ref[...]
        out_ref[:rows] = acc[:, :128].astype(out_ref.dtype)
        out_ref[rows:] = pack(top_ref[...], acc[:, 128:]).astype(out_ref.dtype)


def state_of(ref, rows):
    top, total = unpack(ref[rows:], rows)
    return ref[:rows].astype(jnp.float32), top, total


def merged(first, second):
    numer_a, top_a, total_a = first
    numer_b, top_b, total_b = second
    top = jnp.maximum(top_a, top_b)
    scale_a, scale_b = jnp.exp2(top_a - top), jnp.exp2(top_b - top)
    return numer_a * scale_a + numer_b * scale_b, top, total_a * scale_a + total_b * scale_b


def merge_kernel(rows, got_ref, own_ref, out_ref):
    numer, top, total = merged(state_of(got_ref, rows), state_of(own_ref, rows))
    out_ref[:rows] = numer.astype(out_ref.dtype)
    out_ref[rows:] = pack(top, total).astype(out_ref.dtype)


def finish_kernel(rows, tokens, heads, a_ref, b_ref, own_ref, out_ref):
    numer, top, total = merged(state_of(own_ref, rows), merged(state_of(a_ref, rows), state_of(b_ref, rows)))
    result = (numer / total).astype(out_ref.dtype)
    for h in range(heads):
        out_ref[:, h * HEAD_SIZE : (h + 1) * HEAD_SIZE] = result[h * tokens : (h + 1) * tokens]


def on_device(ctx, queries, new_keys, fresh_values, history_keys, history_values, hist_lens, new_lens):
    tokens, width = queries.shape
    heads = width // HEAD_SIZE
    rows = tokens * heads
    chips = ctx // 2
    me = lax.axis_index("ctx")
    info = jnp.concatenate(
        [hist_lens, new_lens, jnp.stack([me // 2, me % 2]).astype(jnp.int32)]
    )
    swap = [(i, i ^ 1) for i in range(ctx)]

    def moved(array, by):
        return lax.ppermute(array, "ctx", [(i, (i + 2 * by) % ctx) for i in range(ctx)])

    new_both = jnp.concatenate([new_keys, fresh_values], axis=0)
    peer_keys = lax.ppermute(history_keys, "ctx", swap)
    peer_values = lax.ppermute(history_values, "ctx", swap)
    peer_new = lax.ppermute(new_both, "ctx", swap)

    ahead, back = [queries], [queries]
    for step in range(chips // 2):
        ahead.append(moved(ahead[-1], 1))
        if step < chips // 2 - 1:
            back.append(moved(back[-1], -1))

    vmem = pl.BlockSpec(memory_space=pltpu.VMEM)
    smem = pl.BlockSpec(memory_space=pltpu.SMEM)

    def attend(shifts, blocks, kinds):
        count = len(shifts)
        return pl.pallas_call(
            functools.partial(attend_kernel, shifts, tokens, heads, chips),
            out_shape=[jax.ShapeDtypeStruct((rows + STAT_ROWS, 128), kind) for kind in kinds],
            in_specs=[smem] + [vmem] * (count + 6),
            out_specs=[vmem] * count,
            scratch_shapes=[pltpu.VMEM((rows, 128), jnp.float32), pltpu.VMEM((rows, 256), jnp.float32)],
            compiler_params=pltpu.CompilerParams(vmem_limit_bytes=32 * 2**20),
            cost_estimate=pl.CostEstimate(
                flops=count * rows * 4096 * 128 * 2,
                bytes_accessed=2**21,
                transcendentals=0,
            ),
        )(info, *blocks, history_keys, peer_keys, history_values, peer_values, new_both, peer_new)

    def merge(got, own):
        return pl.pallas_call(
            functools.partial(merge_kernel, rows),
            out_shape=jax.ShapeDtypeStruct((rows + STAT_ROWS, 128), jnp.bfloat16),
            in_specs=[vmem] * 2,
            out_specs=vmem,
            compiler_params=pltpu.CompilerParams(vmem_limit_bytes=16 * 2**20),
            cost_estimate=pl.CostEstimate(flops=rows * 1024, bytes_accessed=2**19, transcendentals=0),
        )(got, own)

    f32, bf16 = jnp.float32, jnp.bfloat16
    half = chips // 2
    (own,) = attend((0,), (queries,), (f32,))
    ahead_parts, back_parts = [own], [own]
    for step in range(1, half):
        a, b = attend((-step, step), (ahead[step], back[step]), (f32, bf16 if step == half - 1 else f32))
        ahead_parts.append(a)
        back_parts.append(b)
    (last,) = attend((-half,), (ahead[half],), (bf16,))

    from_ahead, from_back = last, back_parts[half - 1]
    for step in range(half - 1, 0, -1):
        from_ahead = merge(moved(from_ahead, -1), ahead_parts[step])
        if step < half - 1:
            from_back = merge(moved(from_back, 1), back_parts[step])
    from_ahead = moved(from_ahead, -1)
    from_back = moved(from_back, 1)
    return pl.pallas_call(
        functools.partial(finish_kernel, rows, tokens, heads),
        out_shape=jax.ShapeDtypeStruct((tokens, width), jnp.bfloat16),
        in_specs=[vmem] * 3,
        out_specs=vmem,
        compiler_params=pltpu.CompilerParams(vmem_limit_bytes=16 * 2**20),
        cost_estimate=pl.CostEstimate(flops=rows * 2048, bytes_accessed=2**19, transcendentals=0),
    )(from_ahead, from_back, own)


def solution(mesh):
    split = P(("req", "ctx"), "tp")
    return jax.shard_map(
        functools.partial(on_device, mesh.shape["ctx"]),
        mesh=mesh,
        in_specs=(split,) * 5 + (P("req"),) * 2,
        out_specs=split,
        check_vma=False,
    )
```

```python
import functools
import math

import jax
import jax.numpy as jnp
from jax import lax
from jax.experimental import pallas as pl
from jax.experimental.pallas import tpu as pltpu
from jax.sharding import PartitionSpec as P

HEAD_SIZE = 128
REQS = 4
PIECES = 4
FINE = 512
CHUNK = 128
STAT_ROWS = 16
LOG2_SCALE = math.log2(math.e) * HEAD_SIZE**-0.5
NEG = -3.0e38
FLOOR = -(2.0**100)


def ends_of(info, first):
    total = info[first]
    ends = [total]
    for r in range(1, REQS):
        total = total + info[first + r]
        ends.append(total)
    return ends


def request_of(position, ends):
    found = jnp.zeros_like(position)
    for end in ends[:-1]:
        found = found + (position >= end).astype(jnp.int32)
    return found


def pick(request, values):
    result = values[0]
    for r in range(1, len(values)):
        result = jnp.where(request == r, values[r], result)
    return result


def wide(column_block, width):
    if width <= 128:
        return column_block[:, :width]
    return jnp.concatenate([column_block] * (width // 128), axis=1)


def eye():
    rows = lax.broadcasted_iota(jnp.int32, (128, 128), 0)
    return rows == lax.broadcasted_iota(jnp.int32, (128, 128), 1)


def pack(top, total):
    high = total.astype(jnp.bfloat16).astype(jnp.float32)
    low = (total - high).astype(jnp.bfloat16).astype(jnp.float32)
    groups = top.shape[0] // 128
    diagonal = eye()
    at = lax.broadcasted_iota(jnp.int32, (STAT_ROWS, 128), 0)
    stats = jnp.zeros((STAT_ROWS, 128), jnp.float32)
    for kind, source in enumerate((top, high, low)):
        for g in range(groups):
            piece = source[g * 128 : (g + 1) * 128]
            row = jnp.sum(jnp.where(diagonal, piece, 0.0), axis=0, keepdims=True)
            stats = jnp.where(at == kind * groups + g, row, stats)
    return stats


def unpack(stats, rows):
    groups = rows // 128
    diagonal = eye()
    ones = jnp.ones((128, 128), jnp.bfloat16)

    def spread(i):
        row = jnp.broadcast_to(stats[i : i + 1].astype(jnp.float32), (128, 128))
        masked = jnp.where(diagonal, row, 0.0).astype(jnp.bfloat16)
        return jnp.dot(masked, ones, preferred_element_type=jnp.float32)

    top = jnp.concatenate([spread(g) for g in range(groups)], axis=0)
    total = jnp.concatenate([spread(groups + g) + spread(2 * groups + g) for g in range(groups)], axis=0)
    return top, total


def attend_kernel(shift, tokens, heads, chips, info_ref, q_ref, *refs):
    piece_refs, refs = refs[:PIECES], refs[PIECES:]
    out_ref, held_ref, query_ref, top_ref, acc_ref, sems = refs
    rows = tokens * heads
    span = held_ref.shape[1] // 2 - tokens
    chip, core = info_ref[2 * REQS], info_ref[2 * REQS + 1]
    hist_ends, new_ends = ends_of(info_ref, 0), ends_of(info_ref, REQS)
    hist_starts = [jnp.int32(0)] + hist_ends[:-1]

    owner = lax.rem(chip + shift * (2 * core - 1) + chips, chips)
    first_token = (owner * 2 + core) * tokens
    last_token = first_token + (tokens - 1)
    low_request = request_of(first_token, new_ends)
    high_request = request_of(last_token, new_ends)
    low, high = pick(low_request, hist_starts), pick(high_request, hist_ends)

    behind = 2 * lax.rem(chip + (chips - 1), chips)
    beyond = 2 * lax.rem(chip + 1, chips) + 1
    sources = [
        2 * chip + core,
        2 * chip + 1 - core,
        jnp.where(core == 0, behind, beyond),
        jnp.where(core == 0, beyond, behind),
    ]

    def seen(source):
        hist = (source * span < high) & ((source + 1) * span > low)
        last = source * tokens + (tokens - 1)
        fresh = (source * tokens <= last_token) & (request_of(last, new_ends) >= low_request)
        return hist, fresh

    for p in range(PIECES):
        hist, fresh = seen(sources[p])

        @pl.when(hist | fresh)
        def _(p=p):
            pltpu.make_async_copy(piece_refs[p], held_ref.at[p], sems.at[p]).start()

    token = first_token + lax.broadcasted_iota(jnp.int32, (tokens, 1), 0)
    request = request_of(token, new_ends)
    row_low, row_high = pick(request, hist_starts), pick(request, hist_ends)
    for h in range(heads):
        query_ref[h * tokens : (h + 1) * tokens] = q_ref[:, h * HEAD_SIZE : (h + 1) * HEAD_SIZE]
    top_ref[...] = jnp.full((rows, 128), FLOOR, jnp.float32)
    acc_ref[...] = jnp.zeros((rows, 256), jnp.float32)

    def absorb(keys, values, mask):
        count = keys.shape[0]
        both = jnp.concatenate([values, jnp.ones((count, 128), jnp.bfloat16)], axis=1)
        for at in range(0, rows, CHUNK):
            part = pl.ds(at, CHUNK)
            scores = lax.dot_general(
                query_ref[part], keys, (((1,), (1,)), ((), ())), preferred_element_type=jnp.float32
            )
            scores = scores * LOG2_SCALE
            if mask is not None:
                stacked = scores.reshape(CHUNK // tokens, tokens, count)
                scores = jnp.where(mask[None], stacked, NEG).reshape(CHUNK, count)
            most = jnp.max(scores, axis=1, keepdims=True)
            old = top_ref[part]
            new = jnp.maximum(old, most.astype(jnp.bfloat16).astype(jnp.float32))
            weights = jnp.exp2(scores - wide(new, count)).astype(jnp.bfloat16)
            shrink = jnp.exp2(old - new)
            acc_ref[part] = acc_ref[part] * wide(shrink, 256) + jnp.dot(
                weights, both, preferred_element_type=jnp.float32
            )
            top_ref[part] = new

    def piece(p, unused):
        source = pick(p, sources)
        hist, fresh = seen(source)
        base = source * span

        @pl.when(hist | fresh)
        def _():
            pltpu.make_async_copy(piece_refs[0], held_ref.at[p], sems.at[p]).wait()

        whole = (low_request == high_request) & (base >= low) & (base + span <= high)

        @pl.when(whole)
        def _():
            absorb(held_ref[p, :span], held_ref[p, span + tokens : 2 * span + tokens], None)

        @pl.when(hist & jnp.logical_not(whole))
        def _():
            begin = lax.div(jnp.maximum(low - base, 0), FINE)
            end = lax.div(jnp.minimum(high - base, span) + (FINE - 1), FINE)

            def tile(i, same):
                at = pl.multiple_of(i * FINE, FINE)
                position = base + at + lax.broadcasted_iota(jnp.int32, (tokens, FINE), 1)
                mask = (position >= row_low) & (position < row_high)
                absorb(held_ref[p, pl.ds(at, FINE)], held_ref[p, pl.ds(at + (span + tokens), FINE)], mask)
                return same

            lax.fori_loop(begin, end, tile, 0)

        @pl.when(fresh)
        def _():
            position = source * tokens + lax.broadcasted_iota(jnp.int32, (tokens, tokens), 1)
            mask = (position <= token) & (request_of(position, new_ends) == request)
            absorb(held_ref[p, span : span + tokens], held_ref[p, 2 * span + tokens :], mask)

        return unused

    lax.fori_loop(0, PIECES, piece, 0)
    acc = acc_ref[...]
    out_ref[:rows] = acc[:, :128].astype(out_ref.dtype)
    out_ref[rows:] = pack(top_ref[...], acc[:, 128:]).astype(out_ref.dtype)


def state_of(ref, rows):
    top, total = unpack(ref[rows:], rows)
    return ref[:rows].astype(jnp.float32), top, total


def finish_kernel(rows, tokens, heads, *refs):
    out_ref = refs[-1]
    states = [state_of(ref, rows) for ref in refs[:-1]]
    top = functools.reduce(jnp.maximum, [state[1] for state in states])
    numer = total = 0.0
    for part, part_top, part_total in states:
        scale = jnp.exp2(part_top - top)
        numer = numer + part * scale
        total = total + part_total * scale
    result = (numer / total).astype(out_ref.dtype)
    for h in range(heads):
        out_ref[:, h * HEAD_SIZE : (h + 1) * HEAD_SIZE] = result[h * tokens : (h + 1) * tokens]


def on_device(ctx, queries, new_keys, fresh_values, history_keys, history_values, hist_lens, new_lens):
    tokens, width = queries.shape
    span = history_keys.shape[0]
    heads = width // HEAD_SIZE
    rows = tokens * heads
    chips = ctx // 2
    me = lax.axis_index("ctx")
    info = jnp.concatenate([hist_lens, new_lens, jnp.stack([me // 2, me % 2]).astype(jnp.int32)])

    def swapped(array):
        return lax.ppermute(array, "ctx", [(i, i ^ 1) for i in range(ctx)])

    def moved(array, by):
        pairs = [(2 * z + c, 2 * ((z + by * (1 - 2 * c)) % chips) + c) for z in range(chips) for c in range(2)]
        return lax.ppermute(array, "ctx", pairs)

    here = jnp.concatenate([history_keys, new_keys, history_values, fresh_values], axis=0)
    passed = moved(here, 1)
    pieces = (here, swapped(here), passed, swapped(passed))

    vmem = pl.BlockSpec(memory_space=pltpu.VMEM)
    smem = pl.BlockSpec(memory_space=pltpu.SMEM)
    anywhere = pl.BlockSpec(memory_space=pl.ANY)

    def attend(shift, block, kind):
        return pl.pallas_call(
            functools.partial(attend_kernel, shift, tokens, heads, chips),
            out_shape=jax.ShapeDtypeStruct((rows + STAT_ROWS, 128), kind),
            in_specs=[smem, vmem] + [anywhere] * PIECES,
            out_specs=vmem,
            scratch_shapes=[
                pltpu.VMEM((PIECES, 2 * (span + tokens), 128), jnp.bfloat16),
                pltpu.VMEM((rows, 128), jnp.bfloat16),
                pltpu.VMEM((rows, 128), jnp.float32),
                pltpu.VMEM((rows, 256), jnp.float32),
                pltpu.SemaphoreType.DMA((PIECES,)),
            ],
            compiler_params=pltpu.CompilerParams(vmem_limit_bytes=32 * 2**20),
            cost_estimate=pl.CostEstimate(flops=rows * 4096 * 128 * 4, bytes_accessed=2**21, transcendentals=0),
        )(info, block, *pieces)

    reach = chips // 2
    shifts = [reach] + [s for by in range(2, reach, 2) for s in (by, -by)]
    guests = [moved(queries, shift) for shift in shifts]
    parts = [moved(attend(shift, guest, jnp.bfloat16), -shift) for shift, guest in zip(shifts, guests, strict=True)]
    own = attend(0, queries, jnp.float32)
    return pl.pallas_call(
        functools.partial(finish_kernel, rows, tokens, heads),
        out_shape=jax.ShapeDtypeStruct((tokens, width), jnp.bfloat16),
        in_specs=[vmem] * (len(parts) + 1),
        out_specs=vmem,
        compiler_params=pltpu.CompilerParams(vmem_limit_bytes=16 * 2**20),
        cost_estimate=pl.CostEstimate(flops=rows * 2048, bytes_accessed=2**19, transcendentals=0),
    )(own, *parts)


def solution(mesh):
    split = P(("req", "ctx"), "tp")
    return jax.shard_map(
        functools.partial(on_device, mesh.shape["ctx"]),
        mesh=mesh,
        in_specs=(split,) * 5 + (P("req"),) * 2,
        out_specs=split,
        check_vma=False,
    )
```

```python
import functools
import math

import jax
import jax.numpy as jnp
from jax import lax
from jax.experimental import pallas as pl
from jax.experimental.pallas import tpu as pltpu
from jax.sharding import PartitionSpec as P

HEAD_SIZE = 128
REQS = 4
PIECES = 4
CHUNK = 128
STAT_ROWS = 16
LOG2_SCALE = math.log2(math.e) * HEAD_SIZE**-0.5
NEG = -3.0e38
FLOOR = -(2.0**100)


def ends_of(info, first):
    total = info[first]
    ends = [total]
    for r in range(1, REQS):
        total = total + info[first + r]
        ends.append(total)
    return ends


def request_of(position, ends):
    found = jnp.zeros_like(position)
    for end in ends[:-1]:
        found = found + (position >= end).astype(jnp.int32)
    return found


def pick(request, values):
    result = values[0]
    for r in range(1, len(values)):
        result = jnp.where(request == r, values[r], result)
    return result


def wide(column_block, width):
    if width <= 128:
        return column_block[:, :width]
    return jnp.concatenate([column_block] * (width // 128), axis=1)


def eye():
    rows = lax.broadcasted_iota(jnp.int32, (128, 128), 0)
    return rows == lax.broadcasted_iota(jnp.int32, (128, 128), 1)


def pack(top, total):
    high = total.astype(jnp.bfloat16).astype(jnp.float32)
    low = (total - high).astype(jnp.bfloat16).astype(jnp.float32)
    groups = top.shape[0] // 128
    diagonal = eye()
    at = lax.broadcasted_iota(jnp.int32, (STAT_ROWS, 128), 0)
    stats = jnp.zeros((STAT_ROWS, 128), jnp.float32)
    for kind, source in enumerate((top, high, low)):
        for g in range(groups):
            piece = source[g * 128 : (g + 1) * 128]
            row = jnp.sum(jnp.where(diagonal, piece, 0.0), axis=0, keepdims=True)
            stats = jnp.where(at == kind * groups + g, row, stats)
    return stats


def unpack(stats, rows):
    groups = rows // 128
    diagonal = eye()
    ones = jnp.ones((128, 128), jnp.bfloat16)

    def spread(i):
        row = jnp.broadcast_to(stats[i : i + 1].astype(jnp.float32), (128, 128))
        masked = jnp.where(diagonal, row, 0.0).astype(jnp.bfloat16)
        return jnp.dot(masked, ones, preferred_element_type=jnp.float32)

    top = jnp.concatenate([spread(g) for g in range(groups)], axis=0)
    total = jnp.concatenate([spread(groups + g) + spread(2 * groups + g) for g in range(groups)], axis=0)
    return top, total


def attend_kernel(shift, tokens, heads, chips, final, info_ref, q_ref, *refs):
    count_pieces = PIECES // 2
    if final:
        prior_ref, *refs = refs
        fresh_from, refs = refs[:PIECES], refs[PIECES:]
        piece_refs = fresh_from[count_pieces:]
    else:
        piece_refs, refs = refs[:count_pieces], refs[count_pieces:]
    out_ref, held_ref, new_ref, query_ref, score_ref, fresh_ref, top_ref, acc_ref, sems = refs
    rows = tokens * heads
    span = held_ref.shape[1] // 2
    half = span // 2
    chip, core = info_ref[2 * REQS], info_ref[2 * REQS + 1]
    hist_ends, new_ends = ends_of(info_ref, 0), ends_of(info_ref, REQS)
    hist_starts = [jnp.int32(0)] + hist_ends[:-1]

    owner = lax.rem(chip + shift * (2 * core - 1) + chips, chips)
    first_token = (owner * 2 + core) * tokens
    last_token = first_token + (tokens - 1)
    low_request = request_of(first_token, new_ends)
    high_request = request_of(last_token, new_ends)
    low, high = pick(low_request, hist_starts), pick(high_request, hist_ends)

    behind = 2 * lax.rem(chip + (chips - 1), chips)
    beyond = 2 * lax.rem(chip + 1, chips) + 1
    sources = [
        2 * chip + core,
        2 * chip + 1 - core,
        jnp.where(core == 0, behind, beyond),
        jnp.where(core == 0, beyond, behind),
    ]

    def seen(source):
        base = source * span
        first = (base < high) & (base + half > low)
        second = (base + half < high) & (base + span > low)
        last = source * tokens + (tokens - 1)
        fresh = (source * tokens <= last_token) & (request_of(last, new_ends) >= low_request)
        return first, second, fresh

    all_sources = sources
    any_fresh = functools.reduce(jnp.logical_or, [seen(source)[2] for source in all_sources])
    sources = all_sources[count_pieces:] if final else all_sources[:count_pieces]
    found = [seen(source) for source in sources]
    any_hist = functools.reduce(jnp.logical_or, [f | s for f, s, _ in found])
    if not final:
        any_fresh = jnp.bool_(False)

    def fetch(p):
        whole = piece_refs[p]
        return [
            pltpu.make_async_copy(whole.at[pl.ds(0, span)], held_ref.at[p, pl.ds(0, span)], sems.at[0, p]),
            pltpu.make_async_copy(
                whole.at[pl.ds(span + tokens, span)], held_ref.at[p, pl.ds(span, span)], sems.at[1, p]
            ),
        ]

    def fetch_new(p):
        whole = fresh_from[p]
        return [
            pltpu.make_async_copy(
                whole.at[pl.ds(span, tokens)], new_ref.at[0, pl.ds(p * tokens, tokens)], sems.at[2, p]
            ),
            pltpu.make_async_copy(
                whole.at[pl.ds(2 * span + tokens, tokens)], new_ref.at[1, pl.ds(p * tokens, tokens)], sems.at[3, p]
            ),
        ]

    if final:
        @pl.when(any_fresh)
        def _():
            for p in range(PIECES):
                for copy in fetch_new(p):
                    copy.start()

    for p in range(count_pieces):
        @pl.when(found[p][0] | found[p][1])
        def _(p=p):
            for copy in fetch(p):
                copy.start()

    @pl.when(jnp.logical_not(any_hist | any_fresh))
    def _():
        if final:
            out_ref[...] = prior_ref[...].astype(out_ref.dtype)
        else:
            out_ref[:rows] = jnp.zeros((rows, 128), out_ref.dtype)
            at = lax.broadcasted_iota(jnp.int32, (STAT_ROWS, 128), 0)
            out_ref[rows:] = jnp.where(at < rows // 128, FLOOR, 0.0).astype(out_ref.dtype)

    @pl.when(any_hist | any_fresh)
    def _():
        token = first_token + lax.broadcasted_iota(jnp.int32, (tokens, 1), 0)
        request = request_of(token, new_ends)
        row_low, row_high = pick(request, hist_starts), pick(request, hist_ends)
        for h in range(heads):
            query_ref[h * tokens : (h + 1) * tokens] = q_ref[:, h * HEAD_SIZE : (h + 1) * HEAD_SIZE]
        top_ref[...] = jnp.full((rows, 128), NEG, jnp.float32)
        acc_ref[...] = jnp.zeros((rows, 256), jnp.float32)

        def score(keys, mask, into_ref, column):
            count = keys.shape[0]
            for at in range(0, rows, CHUNK):
                part = pl.ds(at, CHUNK)
                scores = lax.dot_general(
                    query_ref[part], keys, (((1,), (1,)), ((), ())), preferred_element_type=jnp.float32
                )
                stacked = scores.reshape(CHUNK // tokens, tokens, count)
                scores = jnp.where(mask[None], stacked, NEG).reshape(CHUNK, count)
                into_ref[part, pl.ds(column, count)] = scores
                most = scores[:, :128]
                for j in range(128, count, 128):
                    most = jnp.maximum(most, scores[:, j : j + 128])
                top_ref[part] = jnp.maximum(top_ref[part], most)

        def weigh(values, from_ref, column):
            count = values.shape[0]
            both = jnp.concatenate([values, jnp.ones((count, 128), jnp.bfloat16)], axis=1)
            for at in range(0, rows, CHUNK):
                part = pl.ds(at, CHUNK)
                scores = from_ref[part, pl.ds(column, count)] * LOG2_SCALE
                weights = jnp.exp2(scores - wide(top_ref[part], count)).astype(jnp.bfloat16)
                acc_ref[part] += jnp.dot(weights, both, preferred_element_type=jnp.float32)

        def over_pieces(work):
            def piece(p, unused):
                source = pick(p, sources)
                first, second, _ = seen(source)
                column = pl.multiple_of(p * span, span)

                @pl.when(first & second)
                def _():
                    work(p, source, 0, span, column)

                @pl.when(first != second)
                def _():
                    skip = pl.multiple_of(jnp.where(first, 0, half), half)
                    work(p, source, skip, half, pl.multiple_of(column + skip, half))

                return unused

            lax.fori_loop(0, count_pieces, piece, 0)

        def score_piece(p, source, skip, count, column):
            position = source * span + skip + lax.broadcasted_iota(jnp.int32, (tokens, count), 1)
            mask = (position >= row_low) & (position < row_high)
            score(held_ref[p, pl.ds(skip, count)], mask, score_ref, column)

        def weigh_piece(p, source, skip, count, column):
            weigh(held_ref[p, pl.ds(span + skip, count)], score_ref, column)

        if final:
            @pl.when(any_fresh)
            def _():
                for p in range(PIECES):
                    for copy in fetch_new(p):
                        copy.wait()
                column = lax.broadcasted_iota(jnp.int32, (tokens, PIECES * tokens), 1)
                position = pick(lax.div(column, tokens), all_sources) * tokens + lax.rem(column, tokens)
                mask = (position <= token) & (request_of(position, new_ends) == request)
                score(new_ref[0], mask, fresh_ref, 0)

        for p in range(count_pieces):
            @pl.when(found[p][0] | found[p][1])
            def _(p=p):
                for copy in fetch(p):
                    copy.wait()

        over_pieces(score_piece)
        top = jnp.max(top_ref[...], axis=1, keepdims=True) * LOG2_SCALE
        top = jnp.maximum(top.astype(jnp.bfloat16).astype(jnp.float32), FLOOR)
        top_ref[...] = jnp.broadcast_to(top, (rows, 128))

        if final:
            @pl.when(any_fresh)
            def _():
                weigh(new_ref[1], fresh_ref, 0)

        over_pieces(weigh_piece)
        state = acc_ref[:, :128], top_ref[...], acc_ref[:, 128:]
        if final:
            state = merged([state, state_of(prior_ref, rows)])
        out_ref[:rows] = state[0].astype(out_ref.dtype)
        out_ref[rows:] = pack(state[1], state[2]).astype(out_ref.dtype)


def state_of(ref, rows):
    top, total = unpack(ref[rows:], rows)
    return ref[:rows].astype(jnp.float32), top, total


def merged(states):
    top = functools.reduce(jnp.maximum, [state[1] for state in states])
    numer = total = 0.0
    for part, part_top, part_total in states:
        scale = jnp.exp2(part_top - top)
        numer = numer + part * scale
        total = total + part_total * scale
    return numer, top, total


def finish_kernel(rows, tokens, heads, *refs):
    out_ref = refs[-1]
    numer, _, total = merged([state_of(ref, rows) for ref in refs[:-1]])
    result = (numer / total).astype(out_ref.dtype)
    for h in range(heads):
        out_ref[:, h * HEAD_SIZE : (h + 1) * HEAD_SIZE] = result[h * tokens : (h + 1) * tokens]


def attend_call(shift, tokens, heads, chips, info, block, prior, pieces, kind):
    rows = tokens * heads
    span = pieces[0].shape[0] // 2 - tokens
    final = prior is not None
    vmem = pl.BlockSpec(memory_space=pltpu.VMEM)
    smem = pl.BlockSpec(memory_space=pltpu.SMEM)
    anywhere = pl.BlockSpec(memory_space=pl.ANY)
    return pl.pallas_call(
        functools.partial(attend_kernel, shift, tokens, heads, chips, final),
        out_shape=jax.ShapeDtypeStruct((rows + STAT_ROWS, 128), kind),
        in_specs=[smem, vmem] + [vmem] * final + [anywhere] * len(pieces),
        out_specs=vmem,
        scratch_shapes=[
            pltpu.VMEM((PIECES // 2, 2 * span, 128), jnp.bfloat16),
            pltpu.VMEM((2, PIECES * tokens, 128), jnp.bfloat16),
            pltpu.VMEM((rows, 128), jnp.bfloat16),
            pltpu.VMEM((rows, PIECES // 2 * span), jnp.float32),
            pltpu.VMEM((rows, PIECES * tokens), jnp.float32),
            pltpu.VMEM((rows, 128), jnp.float32),
            pltpu.VMEM((rows, 256), jnp.float32),
            pltpu.SemaphoreType.DMA((4, PIECES)),
        ],
        compiler_params=pltpu.CompilerParams(vmem_limit_bytes=24 * 2**20),
        cost_estimate=pl.CostEstimate(flops=rows * 4096 * 128 * 4, bytes_accessed=2**21, transcendentals=0),
    )(info, block, *([prior] if final else []), *pieces)


def on_device(ctx, queries, new_keys, fresh_values, history_keys, history_values, hist_lens, new_lens):
    tokens, width = queries.shape
    span = history_keys.shape[0]
    heads = width // HEAD_SIZE
    rows = tokens * heads
    chips = ctx // 2
    me = lax.axis_index("ctx")
    info = jnp.concatenate([hist_lens, new_lens, jnp.stack([me // 2, me % 2]).astype(jnp.int32)])

    def swapped(array):
        return lax.ppermute(array, "ctx", [(i, i ^ 1) for i in range(ctx)])

    def moved(array, by):
        pairs = [(2 * z + c, 2 * ((z + by * (1 - 2 * c)) % chips) + c) for z in range(chips) for c in range(2)]
        return lax.ppermute(array, "ctx", pairs)

    reach = chips // 2
    shifts = [reach] + [s for by in range(2, reach, 2) for s in (by, -by)]
    guests = [moved(queries, shift) for shift in shifts]
    here = jnp.concatenate([history_keys, new_keys, history_values, fresh_values], axis=0)
    near = (here, swapped(here))
    waited = here
    passed = moved(waited, 1)
    vmem = pl.BlockSpec(memory_space=pltpu.VMEM)

    def attend(shift, block, prior, taken, kind):
        return attend_call(shift, tokens, heads, chips, info, block, prior, taken, kind)

    firsts = [attend(shift, block, None, near, jnp.float32) for shift, block in zip(shifts, guests, strict=True)]
    own = attend(0, queries, None, near, jnp.float32)
    passed, own, *firsts = lax.optimization_barrier((passed, own, *firsts))
    pieces = (*near, passed, swapped(passed))
    parts = [
        moved(attend(shift, block, first, pieces, jnp.bfloat16), -shift)
        for shift, block, first in zip(shifts, guests, firsts, strict=True)
    ]
    own = attend(0, queries, own, pieces, jnp.float32)
    return pl.pallas_call(
        functools.partial(finish_kernel, rows, tokens, heads),
        out_shape=jax.ShapeDtypeStruct((tokens, width), jnp.bfloat16),
        in_specs=[vmem] * (len(parts) + 1),
        out_specs=vmem,
        compiler_params=pltpu.CompilerParams(vmem_limit_bytes=16 * 2**20),
        cost_estimate=pl.CostEstimate(flops=rows * 2048, bytes_accessed=2**19, transcendentals=0),
    )(own, *parts)


def solution(mesh):
    split = P(("req", "ctx"), "tp")
    return jax.shard_map(
        functools.partial(on_device, mesh.shape["ctx"]),
        mesh=mesh,
        in_specs=(split,) * 5 + (P("req"),) * 2,
        out_specs=split,
        check_vma=False,
    )
```

```python
import functools
import math

import jax
import jax.numpy as jnp
from jax import lax
from jax.experimental import pallas as pl
from jax.experimental.pallas import tpu as pltpu
from jax.sharding import PartitionSpec as P

HEAD_SIZE = 128
REQS = 4
PIECES = 4
CHUNK = 128
STAT_ROWS = 16
LOG2_SCALE = math.log2(math.e) * HEAD_SIZE**-0.5
NEG = -3.0e38
FLOOR = -(2.0**100)


def ends_of(info, first):
    total = info[first]
    ends = [total]
    for r in range(1, REQS):
        total = total + info[first + r]
        ends.append(total)
    return ends


def request_of(position, ends):
    found = jnp.zeros_like(position)
    for end in ends[:-1]:
        found = found + (position >= end).astype(jnp.int32)
    return found


def pick(request, values):
    result = values[0]
    for r in range(1, len(values)):
        result = jnp.where(request == r, values[r], result)
    return result


def wide(column_block, width):
    if width <= 128:
        return column_block[:, :width]
    return jnp.concatenate([column_block] * (width // 128), axis=1)


def eye():
    rows = lax.broadcasted_iota(jnp.int32, (128, 128), 0)
    return rows == lax.broadcasted_iota(jnp.int32, (128, 128), 1)


def pack(top, total):
    high = total.astype(jnp.bfloat16).astype(jnp.float32)
    low = (total - high).astype(jnp.bfloat16).astype(jnp.float32)
    groups = top.shape[0] // 128
    diagonal = eye()
    at = lax.broadcasted_iota(jnp.int32, (STAT_ROWS, 128), 0)
    stats = jnp.zeros((STAT_ROWS, 128), jnp.float32)
    for kind, source in enumerate((top, high, low)):
        for g in range(groups):
            piece = source[g * 128 : (g + 1) * 128]
            row = jnp.sum(jnp.where(diagonal, piece, 0.0), axis=0, keepdims=True)
            stats = jnp.where(at == kind * groups + g, row, stats)
    return stats


def unpack(stats, rows):
    groups = rows // 128
    diagonal = eye()
    ones = jnp.ones((128, 128), jnp.bfloat16)

    def spread(i):
        row = jnp.broadcast_to(stats[i : i + 1].astype(jnp.float32), (128, 128))
        masked = jnp.where(diagonal, row, 0.0).astype(jnp.bfloat16)
        return jnp.dot(masked, ones, preferred_element_type=jnp.float32)

    top = jnp.concatenate([spread(g) for g in range(groups)], axis=0)
    total = jnp.concatenate([spread(groups + g) + spread(2 * groups + g) for g in range(groups)], axis=0)
    return top, total


def attend_kernel(shift, tokens, heads, chips, priors, info_ref, q_ref, *refs):
    count_pieces = PIECES // 2
    final = priors > 0
    if final:
        prior_refs, refs = refs[:priors], refs[priors:]
        fresh_from, refs = refs[:PIECES], refs[PIECES:]
        piece_refs = fresh_from[count_pieces:]
    else:
        piece_refs, refs = refs[:count_pieces], refs[count_pieces:]
    out_ref, held_ref, new_ref, query_ref, score_ref, fresh_ref, top_ref, acc_ref, sems = refs
    rows = tokens * heads
    span = held_ref.shape[1] // 2
    half = span // 2
    chip, core = info_ref[2 * REQS], info_ref[2 * REQS + 1]
    hist_ends, new_ends = ends_of(info_ref, 0), ends_of(info_ref, REQS)
    hist_starts = [jnp.int32(0)] + hist_ends[:-1]

    owner = lax.rem(chip + shift * (2 * core - 1) + chips, chips)
    first_token = (owner * 2 + core) * tokens
    last_token = first_token + (tokens - 1)
    low_request = request_of(first_token, new_ends)
    high_request = request_of(last_token, new_ends)
    low, high = pick(low_request, hist_starts), pick(high_request, hist_ends)

    behind = 2 * lax.rem(chip + (chips - 1), chips)
    beyond = 2 * lax.rem(chip + 1, chips) + 1
    sources = [
        2 * chip + core,
        2 * chip + 1 - core,
        jnp.where(core == 0, behind, beyond),
        jnp.where(core == 0, beyond, behind),
    ]

    def seen(source):
        base = source * span
        first = (base < high) & (base + half > low)
        second = (base + half < high) & (base + span > low)
        last = source * tokens + (tokens - 1)
        fresh = (source * tokens <= last_token) & (request_of(last, new_ends) >= low_request)
        return first, second, fresh

    all_sources = sources
    any_fresh = functools.reduce(jnp.logical_or, [seen(source)[2] for source in all_sources])
    sources = all_sources[count_pieces:] if final else all_sources[:count_pieces]
    found = [seen(source) for source in sources]
    any_hist = functools.reduce(jnp.logical_or, [f | s for f, s, _ in found])
    if not final:
        any_fresh = jnp.bool_(False)

    def fetch(kind, p, source_ref):
        return pltpu.make_async_copy(
            source_ref.at[pl.ds(kind * (span + tokens), span)],
            held_ref.at[p, pl.ds(kind * span, span)],
            sems.at[kind, p],
        )

    def fetch_new(p):
        whole = fresh_from[p]
        return [
            pltpu.make_async_copy(
                whole.at[pl.ds(span, tokens)], new_ref.at[0, pl.ds(p * tokens, tokens)], sems.at[2, p]
            ),
            pltpu.make_async_copy(
                whole.at[pl.ds(2 * span + tokens, tokens)], new_ref.at[1, pl.ds(p * tokens, tokens)], sems.at[3, p]
            ),
        ]

    if final:
        @pl.when(any_fresh)
        def _():
            for p in range(PIECES):
                for copy in fetch_new(p):
                    copy.start()

    for kind in range(2):
        for p in range(count_pieces):
            @pl.when(found[p][0] | found[p][1])
            def _(kind=kind, p=p):
                fetch(kind, p, piece_refs[p]).start()

    def write(state):
        out_ref[:rows] = state[0].astype(out_ref.dtype)
        out_ref[rows:] = pack(state[1], state[2]).astype(out_ref.dtype)

    @pl.when(jnp.logical_not(any_hist | any_fresh))
    def _():
        if priors == 1:
            out_ref[...] = prior_refs[0][...].astype(out_ref.dtype)
        elif final:
            write(merged([state_of(ref, rows) for ref in prior_refs]))
        else:
            out_ref[:rows] = jnp.zeros((rows, 128), out_ref.dtype)
            at = lax.broadcasted_iota(jnp.int32, (STAT_ROWS, 128), 0)
            out_ref[rows:] = jnp.where(at < rows // 128, FLOOR, 0.0).astype(out_ref.dtype)

    @pl.when(any_hist | any_fresh)
    def _():
        token = first_token + lax.broadcasted_iota(jnp.int32, (tokens, 1), 0)
        request = request_of(token, new_ends)
        row_low, row_high = pick(request, hist_starts), pick(request, hist_ends)
        for h in range(heads):
            query_ref[h * tokens : (h + 1) * tokens] = q_ref[:, h * HEAD_SIZE : (h + 1) * HEAD_SIZE]
        top_ref[...] = jnp.full((rows, 128), NEG, jnp.float32)
        acc_ref[...] = jnp.zeros((rows, 256), jnp.float32)

        def score(keys, mask, into_ref, column):
            count = keys.shape[0]
            for at in range(0, rows, CHUNK):
                part = pl.ds(at, CHUNK)
                scores = lax.dot_general(
                    query_ref[part], keys, (((1,), (1,)), ((), ())), preferred_element_type=jnp.float32
                )
                stacked = scores.reshape(CHUNK // tokens, tokens, count)
                scores = jnp.where(mask[None], stacked, NEG).reshape(CHUNK, count)
                into_ref[part, pl.ds(column, count)] = scores
                most = scores[:, :128]
                for j in range(128, count, 128):
                    most = jnp.maximum(most, scores[:, j : j + 128])
                top_ref[part] = jnp.maximum(top_ref[part], most)

        def weigh(values, from_ref, column):
            count = values.shape[0]
            both = jnp.concatenate([values, jnp.ones((count, 128), jnp.bfloat16)], axis=1)
            for at in range(0, rows, CHUNK):
                part = pl.ds(at, CHUNK)
                scores = from_ref[part, pl.ds(column, count)] * LOG2_SCALE
                weights = jnp.exp2(scores - wide(top_ref[part], count)).astype(jnp.bfloat16)
                acc_ref[part] += jnp.dot(weights, both, preferred_element_type=jnp.float32)

        def over_pieces(work, kind):
            def piece(p, unused):
                source = pick(p, sources)
                first, second, _ = seen(source)
                column = pl.multiple_of(p * span, span)

                @pl.when(first | second)
                def _():
                    fetch(kind, p, piece_refs[0]).wait()

                @pl.when(first & second)
                def _():
                    work(p, source, 0, span, column)

                @pl.when(first != second)
                def _():
                    skip = pl.multiple_of(jnp.where(first, 0, half), half)
                    work(p, source, skip, half, pl.multiple_of(column + skip, half))

                return unused

            lax.fori_loop(0, count_pieces, piece, 0)

        def score_piece(p, source, skip, count, column):
            position = source * span + skip + lax.broadcasted_iota(jnp.int32, (tokens, count), 1)
            mask = (position >= row_low) & (position < row_high)
            score(held_ref[p, pl.ds(skip, count)], mask, score_ref, column)

        def weigh_piece(p, source, skip, count, column):
            weigh(held_ref[p, pl.ds(span + skip, count)], score_ref, column)

        if final:
            @pl.when(any_fresh)
            def _():
                for p in range(PIECES):
                    for copy in fetch_new(p):
                        copy.wait()
                column = lax.broadcasted_iota(jnp.int32, (tokens, PIECES * tokens), 1)
                position = pick(lax.div(column, tokens), all_sources) * tokens + lax.rem(column, tokens)
                mask = (position <= token) & (request_of(position, new_ends) == request)
                score(new_ref[0], mask, fresh_ref, 0)

        over_pieces(score_piece, 0)
        top = jnp.max(top_ref[...], axis=1, keepdims=True) * LOG2_SCALE
        top = jnp.maximum(top.astype(jnp.bfloat16).astype(jnp.float32), FLOOR)
        top_ref[...] = jnp.broadcast_to(top, (rows, 128))

        if final:
            @pl.when(any_fresh)
            def _():
                weigh(new_ref[1], fresh_ref, 0)

        over_pieces(weigh_piece, 1)
        state = acc_ref[:, :128], top_ref[...], acc_ref[:, 128:]
        if final:
            state = merged([state] + [state_of(ref, rows) for ref in prior_refs])
        write(state)


def state_of(ref, rows):
    top, total = unpack(ref[rows:], rows)
    return ref[:rows].astype(jnp.float32), top, total


def merged(states):
    top = functools.reduce(jnp.maximum, [state[1] for state in states])
    numer = total = 0.0
    for part, part_top, part_total in states:
        scale = jnp.exp2(part_top - top)
        numer = numer + part * scale
        total = total + part_total * scale
    return numer, top, total


def finish_kernel(rows, tokens, heads, *refs):
    out_ref = refs[-1]
    numer, _, total = merged([state_of(ref, rows) for ref in refs[:-1]])
    result = (numer / total).astype(out_ref.dtype)
    for h in range(heads):
        out_ref[:, h * HEAD_SIZE : (h + 1) * HEAD_SIZE] = result[h * tokens : (h + 1) * tokens]


def attend_call(shift, tokens, heads, chips, info, block, priors, pieces, kind):
    rows = tokens * heads
    span = pieces[0].shape[0] // 2 - tokens
    count = len(priors)
    vmem = pl.BlockSpec(memory_space=pltpu.VMEM)
    smem = pl.BlockSpec(memory_space=pltpu.SMEM)
    anywhere = pl.BlockSpec(memory_space=pl.ANY)
    return pl.pallas_call(
        functools.partial(attend_kernel, shift, tokens, heads, chips, count),
        out_shape=jax.ShapeDtypeStruct((rows + STAT_ROWS, 128), kind),
        in_specs=[smem, vmem] + [vmem] * count + [anywhere] * len(pieces),
        out_specs=vmem,
        scratch_shapes=[
            pltpu.VMEM((PIECES // 2, 2 * span, 128), jnp.bfloat16),
            pltpu.VMEM((2, PIECES * tokens, 128), jnp.bfloat16),
            pltpu.VMEM((rows, 128), jnp.bfloat16),
            pltpu.VMEM((rows, PIECES // 2 * span), jnp.float32),
            pltpu.VMEM((rows, PIECES * tokens), jnp.float32),
            pltpu.VMEM((rows, 128), jnp.float32),
            pltpu.VMEM((rows, 256), jnp.float32),
            pltpu.SemaphoreType.DMA((4, PIECES)),
        ],
        compiler_params=pltpu.CompilerParams(vmem_limit_bytes=24 * 2**20),
        cost_estimate=pl.CostEstimate(flops=rows * 4096 * 128 * 4, bytes_accessed=2**21, transcendentals=0),
    )(info, block, *priors, *pieces)


def on_device(ctx, queries, new_keys, fresh_values, history_keys, history_values, hist_lens, new_lens):
    tokens, width = queries.shape
    span = history_keys.shape[0]
    heads = width // HEAD_SIZE
    rows = tokens * heads
    chips = ctx // 2
    me = lax.axis_index("ctx")
    info = jnp.concatenate([hist_lens, new_lens, jnp.stack([me // 2, me % 2]).astype(jnp.int32)])

    def swapped(array):
        return lax.ppermute(array, "ctx", [(i, i ^ 1) for i in range(ctx)])

    def moved(array, by):
        pairs = [(2 * z + c, 2 * ((z + by * (1 - 2 * c)) % chips) + c) for z in range(chips) for c in range(2)]
        return lax.ppermute(array, "ctx", pairs)

    here = jnp.concatenate([history_keys, new_keys, history_values, fresh_values], axis=0)
    ahead = moved(queries, 2)
    back = moved(queries, -2)
    here, ahead = lax.optimization_barrier((here, ahead))
    passed = moved(here, 1)
    far = moved(ahead, 2)
    near = (here, swapped(here))
    vmem = pl.BlockSpec(memory_space=pltpu.VMEM)

    def attend(shift, block, priors, taken, kind):
        return attend_call(shift, tokens, heads, chips, info, block, priors, taken, kind)

    f32, bf16 = jnp.float32, jnp.bfloat16
    visits = ((0, queries), (2, ahead), (-2, back))
    own, ahead_part, back_part = [attend(shift, block, (), near, f32) for shift, block in visits]
    passed, own, ahead_part, back_part, far = lax.optimization_barrier((passed, own, ahead_part, back_part, far))
    pieces = (*near, passed, swapped(passed))
    far_part = attend(4, far, (), near, f32)
    far_part = moved(attend(4, far, (far_part,), pieces, bf16), -2)
    back_part = moved(attend(-2, back, (back_part,), pieces, bf16), 2)
    ahead_part = moved(attend(2, ahead, (ahead_part, far_part), pieces, bf16), -2)
    own = attend(0, queries, (own,), pieces, f32)
    parts = (ahead_part, back_part)
    return pl.pallas_call(
        functools.partial(finish_kernel, rows, tokens, heads),
        out_shape=jax.ShapeDtypeStruct((tokens, width), jnp.bfloat16),
        in_specs=[vmem] * (len(parts) + 1),
        out_specs=vmem,
        compiler_params=pltpu.CompilerParams(vmem_limit_bytes=16 * 2**20),
        cost_estimate=pl.CostEstimate(flops=rows * 2048, bytes_accessed=2**19, transcendentals=0),
    )(own, *parts)


def solution(mesh):
    split = P(("req", "ctx"), "tp")
    return jax.shard_map(
        functools.partial(on_device, mesh.shape["ctx"]),
        mesh=mesh,
        in_specs=(split,) * 5 + (P("req"),) * 2,
        out_specs=split,
        check_vma=False,
    )
```

```python
import functools
import math

import jax
import jax.numpy as jnp
from jax import lax
from jax.experimental import pallas as pl
from jax.experimental.pallas import tpu as pltpu
from jax.sharding import PartitionSpec as P

HEAD_SIZE = 128
REQS = 4
PIECES = 4
CHUNK = 128
STAT_ROWS = 16
LOG2_SCALE = math.log2(math.e) * HEAD_SIZE**-0.5
NEG = -3.0e38
FLOOR = -(2.0**100)


def ends_of(info, first):
    total = info[first]
    ends = [total]
    for r in range(1, REQS):
        total = total + info[first + r]
        ends.append(total)
    return ends


def request_of(position, ends):
    found = jnp.zeros_like(position)
    for end in ends[:-1]:
        found = found + (position >= end).astype(jnp.int32)
    return found


def pick(request, values):
    result = values[0]
    for r in range(1, len(values)):
        result = jnp.where(request == r, values[r], result)
    return result


def wide(column_block, width):
    if width <= 128:
        return column_block[:, :width]
    return jnp.concatenate([column_block] * (width // 128), axis=1)


def eye():
    rows = lax.broadcasted_iota(jnp.int32, (128, 128), 0)
    return rows == lax.broadcasted_iota(jnp.int32, (128, 128), 1)


def pack(top, total):
    high = total.astype(jnp.bfloat16).astype(jnp.float32)
    low = (total - high).astype(jnp.bfloat16).astype(jnp.float32)
    groups = top.shape[0] // 128
    diagonal = eye()
    at = lax.broadcasted_iota(jnp.int32, (STAT_ROWS, 128), 0)
    stats = jnp.zeros((STAT_ROWS, 128), jnp.float32)
    for kind, source in enumerate((top, high, low)):
        for g in range(groups):
            piece = source[g * 128 : (g + 1) * 128]
            row = jnp.sum(jnp.where(diagonal, piece, 0.0), axis=0, keepdims=True)
            stats = jnp.where(at == kind * groups + g, row, stats)
    return stats


def unpack(stats, rows):
    groups = rows // 128
    diagonal = eye()
    ones = jnp.ones((128, 128), jnp.bfloat16)

    def spread(i):
        row = jnp.broadcast_to(stats[i : i + 1].astype(jnp.float32), (128, 128))
        masked = jnp.where(diagonal, row, 0.0).astype(jnp.bfloat16)
        return jnp.dot(masked, ones, preferred_element_type=jnp.float32)

    top = jnp.concatenate([spread(g) for g in range(groups)], axis=0)
    total = jnp.concatenate([spread(groups + g) + spread(2 * groups + g) for g in range(groups)], axis=0)
    return top, total


def attend_kernel(shift, tokens, heads, chips, priors, info_ref, q_ref, *refs):
    count_pieces = PIECES // 2
    final = priors > 0
    if final:
        prior_refs, refs = refs[:priors], refs[priors:]
        fresh_from, refs = refs[:PIECES], refs[PIECES:]
        piece_refs = fresh_from[count_pieces:]
    else:
        piece_refs, refs = refs[:count_pieces], refs[count_pieces:]
    out_ref, held_ref, new_ref, query_ref, score_ref, fresh_ref, top_ref, acc_ref, sems = refs
    rows = tokens * heads
    span = held_ref.shape[1] // 2
    half = span // 2
    chip, core = info_ref[2 * REQS], info_ref[2 * REQS + 1]
    hist_ends, new_ends = ends_of(info_ref, 0), ends_of(info_ref, REQS)
    hist_starts = [jnp.int32(0)] + hist_ends[:-1]

    owner = lax.rem(chip + shift * (2 * core - 1) + chips, chips)
    first_token = (owner * 2 + core) * tokens
    last_token = first_token + (tokens - 1)
    low_request = request_of(first_token, new_ends)
    high_request = request_of(last_token, new_ends)
    low, high = pick(low_request, hist_starts), pick(high_request, hist_ends)

    behind = 2 * lax.rem(chip + (chips - 1), chips)
    beyond = 2 * lax.rem(chip + 1, chips) + 1
    sources = [
        2 * chip + core,
        2 * chip + 1 - core,
        jnp.where(core == 0, behind, beyond),
        jnp.where(core == 0, beyond, behind),
    ]

    def seen(source):
        base = source * span
        first = (base < high) & (base + half > low)
        second = (base + half < high) & (base + span > low)
        last = source * tokens + (tokens - 1)
        fresh = (source * tokens <= last_token) & (request_of(last, new_ends) >= low_request)
        return first, second, fresh

    all_sources = sources
    any_fresh = functools.reduce(jnp.logical_or, [seen(source)[2] for source in all_sources])
    sources = all_sources[count_pieces:] if final else all_sources[:count_pieces]
    found = [seen(source) for source in sources]
    any_hist = functools.reduce(jnp.logical_or, [f | s for f, s, _ in found])
    if not final:
        any_fresh = jnp.bool_(False)

    def fetch(kind, p, source_ref):
        return pltpu.make_async_copy(
            source_ref.at[pl.ds(kind * (span + tokens), span)],
            held_ref.at[p, pl.ds(kind * span, span)],
            sems.at[kind, p],
        )

    def fetch_new(p):
        whole = fresh_from[p]
        return [
            pltpu.make_async_copy(
                whole.at[pl.ds(span, tokens)], new_ref.at[0, pl.ds(p * tokens, tokens)], sems.at[2, p]
            ),
            pltpu.make_async_copy(
                whole.at[pl.ds(2 * span + tokens, tokens)], new_ref.at[1, pl.ds(p * tokens, tokens)], sems.at[3, p]
            ),
        ]

    if final:
        @pl.when(any_fresh)
        def _():
            for p in range(PIECES):
                for copy in fetch_new(p):
                    copy.start()

    for kind in range(2):
        for p in range(count_pieces):
            @pl.when(found[p][0] | found[p][1])
            def _(kind=kind, p=p):
                fetch(kind, p, piece_refs[p]).start()

    def write(state):
        out_ref[:rows] = state[0].astype(out_ref.dtype)
        out_ref[rows:] = pack(state[1], state[2]).astype(out_ref.dtype)

    @pl.when(jnp.logical_not(any_hist | any_fresh))
    def _():
        if priors == 1:
            out_ref[...] = prior_refs[0][...].astype(out_ref.dtype)
        elif final:
            write(merged([state_of(ref, rows) for ref in prior_refs]))
        else:
            out_ref[:rows] = jnp.zeros((rows, 128), out_ref.dtype)
            at = lax.broadcasted_iota(jnp.int32, (STAT_ROWS, 128), 0)
            out_ref[rows:] = jnp.where(at < rows // 128, FLOOR, 0.0).astype(out_ref.dtype)

    @pl.when(any_hist | any_fresh)
    def _():
        token = first_token + lax.broadcasted_iota(jnp.int32, (tokens, 1), 0)
        request = request_of(token, new_ends)
        row_low, row_high = pick(request, hist_starts), pick(request, hist_ends)
        for h in range(heads):
            query_ref[h * tokens : (h + 1) * tokens] = q_ref[:, h * HEAD_SIZE : (h + 1) * HEAD_SIZE]
        top_ref[...] = jnp.full((rows, 128), NEG, jnp.float32)
        acc_ref[...] = jnp.zeros((rows, 256), jnp.float32)

        def score(keys, mask, into_ref, column):
            count = keys.shape[0]
            for at in range(0, rows, CHUNK):
                part = pl.ds(at, CHUNK)
                scores = lax.dot_general(
                    query_ref[part], keys, (((1,), (1,)), ((), ())), preferred_element_type=jnp.float32
                )
                stacked = scores.reshape(CHUNK // tokens, tokens, count)
                scores = jnp.where(mask[None], stacked, NEG).reshape(CHUNK, count)
                into_ref[part, pl.ds(column, count)] = scores
                most = scores[:, :128]
                for j in range(128, count, 128):
                    most = jnp.maximum(most, scores[:, j : j + 128])
                top_ref[part] = jnp.maximum(top_ref[part], most)

        def weigh(values, from_ref, column):
            count = values.shape[0]
            both = jnp.concatenate([values, jnp.ones((count, 128), jnp.bfloat16)], axis=1)
            for at in range(0, rows, CHUNK):
                part = pl.ds(at, CHUNK)
                scores = from_ref[part, pl.ds(column, count)] * LOG2_SCALE
                weights = jnp.exp2(scores - wide(top_ref[part], count)).astype(jnp.bfloat16)
                acc_ref[part] += jnp.dot(weights, both, preferred_element_type=jnp.float32)

        def over_pieces(work, kind):
            def piece(p, unused):
                source = pick(p, sources)
                first, second, _ = seen(source)
                column = pl.multiple_of(p * span, span)

                @pl.when(first | second)
                def _():
                    fetch(kind, p, piece_refs[0]).wait()

                @pl.when(first & second)
                def _():
                    work(p, source, 0, span, column)

                @pl.when(first != second)
                def _():
                    skip = pl.multiple_of(jnp.where(first, 0, half), half)
                    work(p, source, skip, half, pl.multiple_of(column + skip, half))

                return unused

            lax.fori_loop(0, count_pieces, piece, 0)

        def score_piece(p, source, skip, count, column):
            position = source * span + skip + lax.broadcasted_iota(jnp.int32, (tokens, count), 1)
            mask = (position >= row_low) & (position < row_high)
            score(held_ref[p, pl.ds(skip, count)], mask, score_ref, column)

        def weigh_piece(p, source, skip, count, column):
            weigh(held_ref[p, pl.ds(span + skip, count)], score_ref, column)

        if final:
            @pl.when(any_fresh)
            def _():
                for p in range(PIECES):
                    for copy in fetch_new(p):
                        copy.wait()
                column = lax.broadcasted_iota(jnp.int32, (tokens, PIECES * tokens), 1)
                position = pick(lax.div(column, tokens), all_sources) * tokens + lax.rem(column, tokens)
                mask = (position <= token) & (request_of(position, new_ends) == request)
                score(new_ref[0], mask, fresh_ref, 0)

        over_pieces(score_piece, 0)
        top = jnp.max(top_ref[...], axis=1, keepdims=True) * LOG2_SCALE
        top = jnp.maximum(top.astype(jnp.bfloat16).astype(jnp.float32), FLOOR)
        top_ref[...] = jnp.broadcast_to(top, (rows, 128))

        if final:
            @pl.when(any_fresh)
            def _():
                weigh(new_ref[1], fresh_ref, 0)

        over_pieces(weigh_piece, 1)
        state = acc_ref[:, :128], top_ref[...], acc_ref[:, 128:]
        if final:
            state = merged([state] + [state_of(ref, rows) for ref in prior_refs])
        write(state)


def state_of(ref, rows):
    top, total = unpack(ref[rows:], rows)
    return ref[:rows].astype(jnp.float32), top, total


def merged(states):
    top = functools.reduce(jnp.maximum, [state[1] for state in states])
    numer = total = 0.0
    for part, part_top, part_total in states:
        scale = jnp.exp2(part_top - top)
        numer = numer + part * scale
        total = total + part_total * scale
    return numer, top, total


def finish_kernel(rows, tokens, heads, *refs):
    out_ref = refs[-1]
    numer, _, total = merged([state_of(ref, rows) for ref in refs[:-1]])
    result = (numer / total).astype(out_ref.dtype)
    for h in range(heads):
        out_ref[:, h * HEAD_SIZE : (h + 1) * HEAD_SIZE] = result[h * tokens : (h + 1) * tokens]


def merge_kernel(rows, own_ref, got_ref, out_ref):
    numer, top, total = merged([state_of(own_ref, rows), state_of(got_ref, rows)])
    out_ref[:rows] = numer.astype(out_ref.dtype)
    out_ref[rows:] = pack(top, total).astype(out_ref.dtype)


def merge_call(rows, own, got):
    vmem = pl.BlockSpec(memory_space=pltpu.VMEM)
    return pl.pallas_call(
        functools.partial(merge_kernel, rows),
        out_shape=jax.ShapeDtypeStruct(got.shape, got.dtype),
        in_specs=[vmem] * 2,
        out_specs=vmem,
        compiler_params=pltpu.CompilerParams(vmem_limit_bytes=16 * 2**20),
        cost_estimate=pl.CostEstimate(flops=rows * 1024, bytes_accessed=2**19, transcendentals=0),
    )(own, got)


def attend_call(shift, tokens, heads, chips, info, block, priors, pieces, kind):
    rows = tokens * heads
    span = pieces[0].shape[0] // 2 - tokens
    count = len(priors)
    vmem = pl.BlockSpec(memory_space=pltpu.VMEM)
    smem = pl.BlockSpec(memory_space=pltpu.SMEM)
    anywhere = pl.BlockSpec(memory_space=pl.ANY)
    return pl.pallas_call(
        functools.partial(attend_kernel, shift, tokens, heads, chips, count),
        out_shape=jax.ShapeDtypeStruct((rows + STAT_ROWS, 128), kind),
        in_specs=[smem, vmem] + [vmem] * count + [anywhere] * len(pieces),
        out_specs=vmem,
        scratch_shapes=[
            pltpu.VMEM((PIECES // 2, 2 * span, 128), jnp.bfloat16),
            pltpu.VMEM((2, PIECES * tokens, 128), jnp.bfloat16),
            pltpu.VMEM((rows, 128), jnp.bfloat16),
            pltpu.VMEM((rows, PIECES // 2 * span), jnp.float32),
            pltpu.VMEM((rows, PIECES * tokens), jnp.float32),
            pltpu.VMEM((rows, 128), jnp.float32),
            pltpu.VMEM((rows, 256), jnp.float32),
            pltpu.SemaphoreType.DMA((4, PIECES)),
        ],
        compiler_params=pltpu.CompilerParams(vmem_limit_bytes=24 * 2**20),
        cost_estimate=pl.CostEstimate(flops=rows * 4096 * 128 * 4, bytes_accessed=2**21, transcendentals=0),
    )(info, block, *priors, *pieces)


def on_device(ctx, queries, new_keys, fresh_values, history_keys, history_values, hist_lens, new_lens):
    tokens, width = queries.shape
    span = history_keys.shape[0]
    heads = width // HEAD_SIZE
    rows = tokens * heads
    chips = ctx // 2
    me = lax.axis_index("ctx")
    info = jnp.concatenate([hist_lens, new_lens, jnp.stack([me // 2, me % 2]).astype(jnp.int32)])

    def swapped(array):
        return lax.ppermute(array, "ctx", [(i, i ^ 1) for i in range(ctx)])

    def moved(array, by):
        pairs = [(2 * z + c, 2 * ((z + by * (1 - 2 * c)) % chips) + c) for z in range(chips) for c in range(2)]
        return lax.ppermute(array, "ctx", pairs)

    here = jnp.concatenate([history_keys, new_keys, history_values, fresh_values], axis=0)
    ahead = moved(queries, 2)
    back = moved(queries, -2)
    here, ahead = lax.optimization_barrier((here, ahead))
    passed = moved(here, 1)
    far = moved(ahead, 2)
    near = (here, swapped(here))
    vmem = pl.BlockSpec(memory_space=pltpu.VMEM)

    def attend(shift, block, priors, taken, kind):
        return attend_call(shift, tokens, heads, chips, info, block, priors, taken, kind)

    f32, bf16 = jnp.float32, jnp.bfloat16
    visits = ((0, queries), (2, ahead), (-2, back))
    own, ahead_part, back_part = [attend(shift, block, (), near, f32) for shift, block in visits]
    passed, own, ahead_part, back_part, far = lax.optimization_barrier((passed, own, ahead_part, back_part, far))
    pieces = (*near, passed, swapped(passed))
    far_part = attend(4, far, (), near, f32)
    far_part = moved(attend(4, far, (far_part,), pieces, bf16), -2)
    back_part = moved(attend(-2, back, (back_part,), pieces, bf16), 2)
    ahead_part = attend(2, ahead, (ahead_part,), pieces, f32)
    ahead_part = moved(merge_call(rows, ahead_part, far_part), -2)
    own = attend(0, queries, (own,), pieces, f32)
    parts = (ahead_part, back_part)
    return pl.pallas_call(
        functools.partial(finish_kernel, rows, tokens, heads),
        out_shape=jax.ShapeDtypeStruct((tokens, width), jnp.bfloat16),
        in_specs=[vmem] * (len(parts) + 1),
        out_specs=vmem,
        compiler_params=pltpu.CompilerParams(vmem_limit_bytes=16 * 2**20),
        cost_estimate=pl.CostEstimate(flops=rows * 2048, bytes_accessed=2**19, transcendentals=0),
    )(own, *parts)


def solution(mesh):
    split = P(("req", "ctx"), "tp")
    return jax.shard_map(
        functools.partial(on_device, mesh.shape["ctx"]),
        mesh=mesh,
        in_specs=(split,) * 5 + (P("req"),) * 2,
        out_specs=split,
        check_vma=False,
    )
```
